256 devices in a mesh: row: 8 (over x, z_hi), col: 32 (over y, z_lo, core).
Axes of the slice: x: 4, y: 4, z: 8 (z_hi: 2, z_lo: 4; z = z_hi * 4 + z_lo), core: 2. Of those that a mesh axis runs over, the one named last changes fastest.
Arguments:
- amplitudes: bfloat16 [8192, 65536], P('row', 'col'), may hold values from -6 to 6
- residual_in: bfloat16 [8192, 65536], P('row', 'col'), may hold values from -6 to 6
- cholesky: bfloat16 [65536, 1280], P('col', 'row'), may hold values from -0.0625 to 0.0625
Outputs:
- residual_out: bfloat16 [8192, 65536], P('row', 'col')
The draws below stay inside these ranges and needn't reach their ends.
All inputs are finite; a program needn't handle non-finite values.
Results may differ from the reference program's by a relative error of at most 0.004.
Values may be sent and summed in bfloat16 or wider, within the bound.
A program may use at most 64 MiB of HBM per device.

```python
import jax
import jax.numpy as jnp
from jax import lax

JB = 65536
NVEC = 1280
ROWS = 8192


def block_scale(own_key, extent, cuts, low, top_value):
    gain = 1.0
    for dim, shards_of in cuts:
        draws = jax.random.uniform(jax.random.fold_in(jax.random.fold_in(own_key, 6), dim), (shards_of,), jnp.float32, low / len(cuts), top_value / len(cuts))
        gain = gain * jnp.repeat(jnp.exp(draws), extent[dim] // shards_of).reshape((-1,) + (1,) * (len(extent) - 1 - dim))
    return gain


def gaussian(key, dims, deviation, reach, pieces=(), kind=jnp.bfloat16):
    values = deviation * jax.random.normal(key, dims, jnp.float32)
    if pieces:
        values = values * block_scale(key, dims, pieces, -0.22, 0.18)
    return jnp.clip(values, -reach, reach).astype(kind)


def setup_inputs(seed: int = 0) -> dict:
    key_of = jax.random.split(jax.random.key(seed), 4)
    amplitudes = gaussian(key_of[0], (ROWS, JB), 1.0, 6.0, ((0, 8), (1, 32)))
    residual_in = gaussian(key_of[1], (ROWS, JB), 1.0, 6.0, ((0, 8), (1, 32)))
    cholesky = gaussian(key_of[2], (JB, NVEC), (JB // 8) ** -0.5, 0.0625, ((0, 32), (1, 8)))
    return {"amplitudes": amplitudes, "residual_in": residual_in, "cholesky": cholesky}


def reference(amplitudes, residual_in, cholesky):
    chi_sum = jnp.dot(amplitudes, cholesky, preferred_element_type=jnp.float32)
    chi = chi_sum.astype(jnp.bfloat16)
    update = lax.dot_general(chi, cholesky, (((1,), (1,)), ((), ())), preferred_element_type=jnp.float32)
    return (residual_in.astype(jnp.float32) + update).astype(jnp.bfloat16)
```

```python
import functools

import jax
import jax.numpy as jnp
from jax import lax
from jax.experimental import pallas as pl
from jax.experimental.pallas import tpu as pltpu
from jax.sharding import PartitionSpec as P

MESH = pl.DeviceIdType.MESH
BF16, F32 = jnp.bfloat16, jnp.float32

ROWS, COLS, VEC = 1024, 2048, 1280
SHARD = 160
SUBS, SUB = 5, 32
LANES = 128

ARRIVAL = (
    [(0, 0), (0, 1), (0, 2), (0, 3)]
    + [(0, 4), (1, 0), (2, 4), (1, 1), (2, 3), (1, 2), (2, 2), (1, 3), (2, 1), (1, 4), (2, 0), (4, 0)]
    + [(3, 0), (3, 4), (4, 1), (3, 1), (3, 3), (5, 0), (6, 0), (4, 2), (3, 2), (4, 3)]
    + [(5, 1), (6, 1), (5, 2), (6, 2), (4, 4), (7, 0), (5, 3), (6, 3)]
    + [(7, 1), (7, 2), (7, 3), (5, 4), (6, 4), (7, 4)]
)
PLACE = {piece: i * SUB for i, piece in enumerate(ARRIVAL)}
CHUNKS = ((4, False), (12, False), (10, False), (8, False), (6, True))
STARTS = [sum(n for n, _ in CHUNKS[:i]) for i in range(len(CHUNKS))]
GROUPS = ((0, 1), (2,), (3,), (4,))
ON_RIGHT = {1: (0, 1, 2), 5: (0, 1)}


def first_row(chunk):
    return STARTS[chunk] * SUB


def height(chunk):
    return CHUNKS[chunk][0] * SUB


def body(
    a_hbm, r_hbm, c_hbm, o_hbm,
    a, res, cv, panel, acc, chi, chit, own, sib_out, sib_in, y_out, y_in, y_sum, z_out, z_in,
    local_sem, out_sem, zx_s, zx_r, x_s, x_r, f_s, f_r, core_s, core_r, y_s, y_r, z_s, z_r, zg_s, zg_r, g_s, g_r, t_s,
):
    row, col = lax.axis_index("row"), lax.axis_index("col")
    y, zl, core = col // 8, lax.rem(col // 2, 4), lax.rem(col, 2)
    other = 1 - core

    def at(y, zl, core):
        return (row, (y * 4 + zl) * 2 + core)

    right, left = (lax.rem(row + 2, 8), col), (lax.rem(row + 6, 8), col)
    across = (row + 1 - 2 * lax.rem(row, 2), col)
    sibling = at(y, zl, other)
    ys = [lax.rem(y + d, 4) for d in range(4)]
    ys_back = [lax.rem(y + 4 - d, 4) for d in range(4)]
    zs = [lax.rem(zl + e, 4) for e in range(4)]
    partners = [right, left, across, sibling]
    partners += [at(ys[d], zl, core) for d in (1, 2, 3)]
    partners += [at(ys[d], zl, other) for d in (1, 2, 3)]
    partners += [at(y, zs[e], core) for e in (1, 2, 3)]

    barrier = pltpu.get_barrier_semaphore()
    for device in partners:
        pl.semaphore_signal(barrier, inc=1, device_id=device, device_id_type=MESH)
    load_c = pltpu.make_async_copy(c_hbm, cv, local_sem.at[0])
    load_a = pltpu.make_async_copy(a_hbm, a, local_sem.at[1])
    load_r = pltpu.make_async_copy(r_hbm, res, local_sem.at[2])
    load_c.start()
    load_a.start()
    load_r.start()
    load_c.wait()
    for piece in range(4):
        s = pl.ds(piece * 512, 512)
        turned = cv[s, :].T
        for j in range(SUBS):
            panel[pl.ds(PLACE[0, j], SUB), s] = turned[j * SUB : (j + 1) * SUB, :]
    pl.semaphore_wait(barrier, len(partners))

    unsent = []

    def send(src, dst, send_sem, recv_sem, device):
        copy = pltpu.make_async_remote_copy(
            src_ref=src, dst_ref=dst, send_sem=send_sem, recv_sem=recv_sem, device_id=device, device_id_type=MESH
        )
        copy.start()
        unsent.append(copy)
        return copy

    arriving = {}

    def move(piece, to, send_sem, recv_sem, device):
        arriving[to] = send(
            panel.at[pl.ds(PLACE[piece], SUB), :], panel.at[pl.ds(PLACE[to], SUB), :], send_sem, recv_sem, device
        )

    def need(piece):
        if piece in arriving:
            arriving.pop(piece).wait_recv()

    def both_ways(block, j, jl):
        which = block // 4
        move((block, j), (block + 1, j), x_s.at[which, 0, j], x_r.at[which, 0, j], right)
        move((block, jl), (block + 2, jl), x_s.at[which, 1, jl], x_r.at[which, 1, jl], left)

    def pass_on(block, j):
        need((block, j))
        base = 1 if block < 4 else 5
        goes_right = j in ON_RIGHT[base]
        if goes_right == (block == base):
            device = right if goes_right else left
            move((block, j), (base + 2, j), f_s.at[base // 4, j], f_r.at[base // 4, j], device)

    def from_across(j):
        need((4, j))
        both_ways(4, j, j)

    def multiply(c):
        n, direct = CHUNKS[c]
        for piece in ARRIVAL[STARTS[c] : STARTS[c] + n]:
            need(piece)
        rows = pl.ds(first_row(c), height(c))

        def half(which, into):
            for t in range(2):
                s = pl.ds(pl.multiple_of(which * 512 + t * 256, 256), 256)
                part = lax.dot_general(panel[rows, :], a[s, :], (((1,), (1,)), ((), ())), preferred_element_type=F32)
                for u in range(2):
                    tile = part[:, u * LANES : (u + 1) * LANES]
                    into[2 * t + u, rows, :] = tile
                    if direct:
                        y_out[which * 4 + 2 * t + u, rows, :] = tile.astype(BF16)

        half(other, sib_out)
        if direct:
            for d in (2, 1, 3, 0):
                send(
                    y_out.at[other * 4 + ys[d], rows, :], y_in.at[4 + d, rows, :],
                    y_s.at[c, 4 + d], y_r.at[c, 4 + d], at(ys[d], zl, other),
                )
        else:
            core_copies[c] = send(sib_out.at[:, rows, :], sib_in.at[:, rows, :], core_s.at[c], core_r.at[c], sibling)
        half(core, own)
        if direct:
            for d in (2, 1, 3):
                send_y(c, rows, d)

    core_copies = {}

    def recv(dst, sem):
        return pltpu.make_async_remote_copy(
            src_ref=dst, dst_ref=dst, send_sem=sem, recv_sem=sem, device_id=sibling, device_id_type=MESH
        )

    def send_y(c, rows, d):
        send(
            y_out.at[core * 4 + ys[d], rows, :], y_in.at[d, rows, :],
            y_s.at[c, d], y_r.at[c, d], at(ys[d], zl, core),
        )

    def scatter_y(c):
        if CHUNKS[c][1]:
            return
        rows = pl.ds(first_row(c), height(c))
        core_copies[c].wait_recv()
        for d in (2, 1, 3, 0):
            total = own[ys[d], rows, :] + sib_in[ys[d], rows, :]
            if d:
                y_out[core * 4 + ys[d], rows, :] = total.astype(BF16)
                send_y(c, rows, d)
            else:
                own[y, rows, :] = total

    def scatter_z(c):
        rows = pl.ds(first_row(c), height(c))
        part = height(c) // 4
        total = own[y, rows, :]
        for d in (1, 3, 2, 4, 5, 7, 6) if CHUNKS[c][1] else (1, 3, 2):
            recv(y_in.at[d, rows, :], y_r.at[c, d]).wait_recv()
            total = total + y_in[d, rows, :].astype(F32)
        y_sum[rows, :] = total
        z_out[rows, :] = total.astype(BF16)
        for e in (3, 2, 1):
            src = pl.ds(pl.multiple_of(first_row(c) + part * zs[e], 16), part)
            dst = pl.ds(first_row(c) // 4, part)
            send(z_out.at[src, :], z_in.at[e, dst, :], z_s.at[c, e], z_r.at[c, e], at(y, zs[e], core))

    def gather_z(c):
        part = height(c) // 4
        mine = pl.ds(pl.multiple_of(first_row(c) + part * zl, 16), part)
        total = y_sum[mine, :]
        for e in (1, 2, 3):
            slot = pl.ds(first_row(c) // 4, part)
            recv(z_in.at[e, slot, :], z_r.at[c, e]).wait_recv()
            total = total + z_in[e, slot, :].astype(F32)
        tile = core * 4 + y
        chi[tile, mine, :] = total.astype(BF16)
        for e in (3, 2, 1):
            piece = chi.at[tile, mine, :]
            send(piece, piece, zg_s.at[c, e], zg_r.at[c, e], at(y, zs[e], core))

    def gather_y(c):
        rows = pl.ds(first_row(c), height(c))
        part = height(c) // 4
        tile = chi.at[core * 4 + y, rows, :]
        for e in (1, 2, 3):
            theirs = pl.ds(pl.multiple_of(first_row(c) + part * lax.rem(zl + 4 - e, 4), 16), part)
            recv(chi.at[core * 4 + y, theirs, :], zg_r.at[c, e]).wait_recv()
        for d in (2, 1, 3):
            send(tile, tile, g_s.at[c, d], g_r.at[c, d], at(ys[d], zl, core))
            if CHUNKS[c][1]:
                send(tile, tile, g_s.at[c, 4 + d], g_r.at[c, 4 + d], at(ys[d], zl, other))
        send(tile, tile, g_s.at[c, 4], g_r.at[c, 4], sibling)

    def gather_core(c):
        rows = pl.ds(first_row(c), height(c))
        for d in (1, 3, 2):
            tile = chi.at[core * 4 + ys_back[d], rows, :]
            recv(tile, g_r.at[c, d]).wait_recv()
            if not CHUNKS[c][1]:
                send(tile, tile, g_s.at[c, 4 + d], g_r.at[c, 4 + d], sibling)

    def multiply_back(g):
        group = GROUPS[g]
        for c in group:
            for d in (0, 1, 3, 2):
                tile = chi.at[other * 4 + ys_back[d], pl.ds(first_row(c), height(c)), :]
                recv(tile, g_r.at[c, 4 + d]).wait_recv()
        rows = pl.ds(first_row(group[0]), sum(height(c) for c in group))
        depth = sum(height(c) for c in group)
        for t in range(8):
            chit[pl.ds(t * LANES, LANES), pl.ds(0, depth)] = chi[t, rows, :].T
        last = g == len(GROUPS) - 1

        @pl.loop(0, COLS // 256)
        def _(i):
            s = pl.ds(pl.multiple_of(i * 256, 256), 256)
            update = jnp.dot(chit[:, pl.ds(0, depth)], panel[rows, s], preferred_element_type=F32)
            if last:
                res[:, s] = (res[:, s].astype(F32) + (acc[:, s] + update)).astype(BF16)
                pltpu.make_async_copy(res.at[:, s], o_hbm.at[:, s], out_sem.at[i]).start()
            elif g == 0:
                acc[:, s] = update
            else:
                acc[:, s] += update

    steps = []

    def when(time, step, *args):
        steps.append((time, len(steps), functools.partial(step, *args)))

    for j in range(SUBS):
        when(6 * (j + 1), from_across, j)
        when(3 * (j + 1), pass_on, 1, j)
        when(3 * (j + 1), pass_on, 2, SUBS - 1 - j)
        when((23, 29, 32, 36, 39)[j], pass_on, 5, j)
        when((23, 29, 32, 36, 39)[j], pass_on, 6, j)
    ready = (0.5, 16, 26, 36, 43)
    for c, start in enumerate(ready):
        for delay, step in enumerate((multiply, scatter_y, scatter_z, gather_z, gather_y, gather_core)):
            when(start + (0, 3, 6, 9, 12, 15)[delay], step, c)
    for g, group in enumerate(GROUPS):
        when(ready[group[-1]] + 17, multiply_back, g)

    for j in range(SUBS):
        move((0, j), (4, j), zx_s.at[j], zx_r.at[j], across)
    for j in range(SUBS):
        both_ways(0, j, SUBS - 1 - j)
    load_a.wait()
    load_r.wait()
    for _, _, step in sorted(steps, key=lambda s: s[:2]):
        step()
    for copy in unsent:
        copy.wait_send()
    for i in range(COLS // 256):
        s = pl.ds(i * 256, 256)
        pltpu.make_async_copy(res.at[:, s], o_hbm.at[:, s], out_sem.at[i]).wait()


def cycle_term(amplitudes, residual_in, cholesky):
    dma = pltpu.SemaphoreType.DMA
    n = len(CHUNKS)
    depth = max(sum(height(c) for c in g) for g in GROUPS)
    any_space = pl.BlockSpec(memory_space=pl.ANY)
    return pl.pallas_call(
        body,
        name="cycle_term",
        out_shape=jax.ShapeDtypeStruct((ROWS, COLS), BF16),
        in_specs=[any_space] * 3,
        out_specs=any_space,
        scratch_shapes=[
            pltpu.VMEM((ROWS, COLS), BF16),
            pltpu.VMEM((ROWS, COLS), BF16),
            pltpu.VMEM((COLS, SHARD), BF16),
            pltpu.VMEM((VEC, COLS), BF16),
            pltpu.VMEM((ROWS, COLS), F32),
            pltpu.VMEM((8, VEC, LANES), BF16),
            pltpu.VMEM((ROWS, depth), BF16),
            pltpu.VMEM((4, VEC, LANES), F32),
            pltpu.VMEM((4, VEC, LANES), F32),
            pltpu.VMEM((4, VEC, LANES), F32),
            pltpu.VMEM((8, VEC, LANES), BF16),
            pltpu.VMEM((8, VEC, LANES), BF16),
            pltpu.VMEM((VEC, LANES), F32),
            pltpu.VMEM((VEC, LANES), BF16),
            pltpu.VMEM((4, VEC // 4, LANES), BF16),
            dma((3,)), dma((COLS // 256,)),
            dma((SUBS,)), dma((SUBS,)),
            dma((2, 2, SUBS)), dma((2, 2, SUBS)),
            dma((2, SUBS)), dma((2, SUBS)),
            dma((n,)), dma((n,)),
            dma((n, 8)), dma((n, 8)),
            dma((n, 4)), dma((n, 4)),
            dma((n, 4)), dma((n, 4)),
            dma((n, 8)), dma((n, 8)),
            dma((1,)),
        ],
        compiler_params=pltpu.CompilerParams(collective_id=0, has_side_effects=True, vmem_limit_bytes=56 << 20),
        cost_estimate=pl.CostEstimate(flops=4 * ROWS * COLS * VEC, bytes_accessed=14 << 20, transcendentals=0),
    )(amplitudes, residual_in, cholesky)


def solution(mesh):
    in_specs = (P("row", "col"), P("row", "col"), P("col", "row"))
    out_specs = P("row", "col")
    return jax.shard_map(cycle_term, mesh=mesh, in_specs=in_specs, out_specs=out_specs, check_vma=False)
```

```python
import functools

import jax
import jax.numpy as jnp
from jax import lax
from jax.experimental import pallas as pl
from jax.experimental.pallas import tpu as pltpu
from jax.sharding import PartitionSpec as P

MESH = pl.DeviceIdType.MESH
BF16, F32 = jnp.bfloat16, jnp.float32

ROWS, COLS, VEC = 1024, 2048, 1280
SHARD = 160
SUBS, SUB = 5, 32
LANES = 128

ARRIVAL = (
    [(0, 0), (0, 1), (0, 2), (0, 3), (0, 4), (1, 0), (2, 4), (1, 1)]
    + [(2, 3), (1, 2), (2, 2), (1, 3), (2, 1), (1, 4), (2, 0), (4, 0)]
    + [(4, 1), (3, 0), (3, 4), (3, 1), (4, 2), (5, 0), (6, 0), (3, 3)]
    + [(3, 2), (4, 3), (5, 1), (6, 1), (5, 2), (6, 2), (6, 3), (4, 4)]
    + [(7, 0), (7, 2), (5, 3), (6, 4)]
    + [(7, 1), (7, 3)]
    + [(5, 4), (7, 4)]
)
PLACE = {piece: i * SUB for i, piece in enumerate(ARRIVAL)}
CHUNKS = (
    (8, False, False), (8, False, False), (8, False, False), (8, False, False),
    (4, False, True), (2, True, True), (2, True, True),
)
STARTS = [sum(chunk[0] for chunk in CHUNKS[:i]) for i in range(len(CHUNKS))]
GROUPS = ((0,), (1,), (2,), (3,), (4, 5, 6))
PARTS = 4
SLICES, SLICE = 10, 16
ON_RIGHT = {1: (0, 1, 2), 5: (0, 1)}


def first_row(chunk):
    return STARTS[chunk] * SUB


def height(chunk):
    return CHUNKS[chunk][0] * SUB


def body(
    a_hbm, r_hbm, c_hbm, out,
    a, res, panel, acc, chi, own, sib_out, sib_in, y_out, y_in, y_sum, z_out, z_in,
    local_sem, own_sem, zx_s, zx_r, x_s, x_r, f_s, f_r, core_s, core_r, y_s, y_r, z_s, z_r, zg_s, zg_r, g_s, g_r,
):
    row, col = lax.axis_index("row"), lax.axis_index("col")
    y, zl, core = col // 8, lax.rem(col // 2, 4), lax.rem(col, 2)
    other = 1 - core

    def at(y, zl, core):
        return (row, (y * 4 + zl) * 2 + core)

    right, left = (lax.rem(row + 2, 8), col), (lax.rem(row + 6, 8), col)
    across = (row + 1 - 2 * lax.rem(row, 2), col)
    sibling = at(y, zl, other)
    ys = [lax.rem(y + d, 4) for d in range(4)]
    ys_back = [lax.rem(y + 4 - d, 4) for d in range(4)]
    zs = [lax.rem(zl + e, 4) for e in range(4)]
    partners = [right, left, across, sibling]
    partners += [at(ys[d], zl, core) for d in (1, 2, 3)]
    partners += [at(ys[d], zl, other) for d in (1, 2, 3)]
    partners += [at(y, zs[e], core) for e in (1, 2, 3)]

    barrier = pltpu.get_barrier_semaphore()
    for device in partners:
        pl.semaphore_signal(barrier, inc=1, device_id=device, device_id_type=MESH)
    load_c = [
        pltpu.make_async_copy(c_hbm.at[pl.ds(j * SUB, SUB), :], panel.at[pl.ds(PLACE[0, j], SUB), :], own_sem.at[j])
        for j in range(SUBS)
    ]
    load_a = pltpu.make_async_copy(a_hbm, a, local_sem.at[0])
    load_r = pltpu.make_async_copy(r_hbm, res, local_sem.at[1])
    for load in load_c:
        load.start()
    load_a.start()
    load_r.start()
    for load in load_c:
        load.wait()
    pl.semaphore_wait(barrier, len(partners))

    unsent = []

    def send(src, dst, send_sem, recv_sem, device):
        copy = pltpu.make_async_remote_copy(
            src_ref=src, dst_ref=dst, send_sem=send_sem, recv_sem=recv_sem, device_id=device, device_id_type=MESH
        )
        copy.start()
        unsent.append(copy)
        return copy

    arriving = {}

    def move(piece, to, send_sem, recv_sem, device):
        arriving[to] = send(
            panel.at[pl.ds(PLACE[piece], SUB), :], panel.at[pl.ds(PLACE[to], SUB), :], send_sem, recv_sem, device
        )

    def need(piece):
        if piece in arriving:
            arriving.pop(piece).wait_recv()

    crossing = []

    def cross(count):
        for i in range(len(crossing), len(crossing) + count):
            j, offset = i * SLICE // SUB, i * SLICE % SUB
            src, dst = (pl.ds(PLACE[block, j] + offset, SLICE) for block in (0, 4))
            crossing.append(send(panel.at[src, :], panel.at[dst, :], zx_s.at[i], zx_r.at[i], across))

    def crossed(i):
        crossing[i].wait_recv()
        j, offset = i * SLICE // SUB, i * SLICE % SUB
        if offset + SLICE == SUB:
            both_ways(4, j, j)

    def both_ways(block, j, jl):
        which = block // 4
        move((block, j), (block + 1, j), x_s.at[which, 0, j], x_r.at[which, 0, j], right)
        move((block, jl), (block + 2, jl), x_s.at[which, 1, jl], x_r.at[which, 1, jl], left)

    def pass_on(block, j):
        need((block, j))
        base = 1 if block < 4 else 5
        goes_right = j in ON_RIGHT[base]
        if goes_right == (block == base):
            device = right if goes_right else left
            move((block, j), (base + 2, j), f_s.at[base // 4, j], f_r.at[base // 4, j], device)

    def multiply(c):
        n, direct, _ = CHUNKS[c]
        for piece in ARRIVAL[STARTS[c] : STARTS[c] + n]:
            need(piece)
        rows = pl.ds(first_row(c), height(c))

        def half(which, into):
            s = pl.ds(pl.multiple_of(which * 512, 512), 512)
            part = lax.dot_general(panel[rows, :], a[s, :], (((1,), (1,)), ((), ())), preferred_element_type=F32)
            for t in range(4):
                tile = part[:, t * LANES : (t + 1) * LANES]
                into[t, rows, :] = tile
                if direct:
                    y_out[which * 4 + t, rows, :] = tile.astype(BF16)

        half(other, sib_out)
        if direct:
            for d in (2, 1, 3, 0):
                send(
                    y_out.at[other * 4 + ys[d], rows, :], y_in.at[4 + d, rows, :],
                    y_s.at[c, 4 + d], y_r.at[c, 4 + d], at(ys[d], zl, other),
                )
        else:
            core_copies[c] = send(sib_out.at[:, rows, :], sib_in.at[:, rows, :], core_s.at[c], core_r.at[c], sibling)
        half(core, own)
        if direct:
            for d in (2, 1, 3):
                send_y(c, rows, d)

    core_copies = {}

    def recv(dst, sem):
        return pltpu.make_async_remote_copy(
            src_ref=dst, dst_ref=dst, send_sem=sem, recv_sem=sem, device_id=sibling, device_id_type=MESH
        )

    def send_y(c, rows, d):
        send(
            y_out.at[core * 4 + ys[d], rows, :], y_in.at[d, rows, :],
            y_s.at[c, d], y_r.at[c, d], at(ys[d], zl, core),
        )

    def scatter_y(c):
        if CHUNKS[c][1]:
            return
        rows = pl.ds(first_row(c), height(c))
        core_copies[c].wait_recv()
        for d in (2, 1, 3, 0):
            total = own[ys[d], rows, :] + sib_in[ys[d], rows, :]
            if d:
                y_out[core * 4 + ys[d], rows, :] = total.astype(BF16)
                send_y(c, rows, d)
            else:
                own[y, rows, :] = total

    def scatter_z(c):
        rows = pl.ds(first_row(c), height(c))
        part = height(c) // 4
        total = own[y, rows, :]
        for d in (1, 3, 2, 4, 5, 7, 6) if CHUNKS[c][1] else (1, 3, 2):
            recv(y_in.at[d, rows, :], y_r.at[c, d]).wait_recv()
            total = total + y_in[d, rows, :].astype(F32)
        y_sum[rows, :] = total
        z_out[rows, :] = total.astype(BF16)
        if CHUNKS[c][2]:
            for e in (3, 2, 1):
                send(z_out.at[rows, :], z_in.at[e, rows, :], z_s.at[c, e], z_r.at[c, e], at(y, zs[e], core))
            return
        for e in (3, 2, 1):
            src = pl.ds(pl.multiple_of(first_row(c) + part * zs[e], 16), part)
            dst = pl.ds(first_row(c) // 4, part)
            send(z_out.at[src, :], z_in.at[e, dst, :], z_s.at[c, e], z_r.at[c, e], at(y, zs[e], core))

    def gather_z(c):
        if CHUNKS[c][2]:
            return
        part = height(c) // 4
        mine = pl.ds(pl.multiple_of(first_row(c) + part * zl, 16), part)
        total = y_sum[mine, :]
        for e in (1, 2, 3):
            slot = pl.ds(first_row(c) // 4, part)
            recv(z_in.at[e, slot, :], z_r.at[c, e]).wait_recv()
            total = total + z_in[e, slot, :].astype(F32)
        tile = core * 4 + y
        chi[tile, mine, :] = total.astype(BF16)
        for e in (3, 2, 1):
            piece = chi.at[tile, mine, :]
            send(piece, piece, zg_s.at[c, e], zg_r.at[c, e], at(y, zs[e], core))

    def gather_y(c):
        rows = pl.ds(first_row(c), height(c))
        part = height(c) // 4
        tile = chi.at[core * 4 + y, rows, :]
        if CHUNKS[c][2]:
            total = y_sum[rows, :]
            for e in (1, 2, 3):
                recv(z_in.at[e, rows, :], z_r.at[c, e]).wait_recv()
                total = total + z_in[e, rows, :].astype(F32)
            chi[core * 4 + y, rows, :] = total.astype(BF16)
        for e in () if CHUNKS[c][2] else (1, 2, 3):
            theirs = pl.ds(pl.multiple_of(first_row(c) + part * lax.rem(zl + 4 - e, 4), 16), part)
            recv(chi.at[core * 4 + y, theirs, :], zg_r.at[c, e]).wait_recv()
        for d in (2, 1, 3):
            send(tile, tile, g_s.at[c, d], g_r.at[c, d], at(ys[d], zl, core))
            if CHUNKS[c][1]:
                send(tile, tile, g_s.at[c, 4 + d], g_r.at[c, 4 + d], at(ys[d], zl, other))
        send(tile, tile, g_s.at[c, 4], g_r.at[c, 4], sibling)

    def gather_core(c):
        rows = pl.ds(first_row(c), height(c))
        for d in (1, 3, 2):
            tile = chi.at[core * 4 + ys_back[d], rows, :]
            recv(tile, g_r.at[c, d]).wait_recv()
            if not CHUNKS[c][1]:
                send(tile, tile, g_s.at[c, 4 + d], g_r.at[c, 4 + d], sibling)

    def multiply_back(g, part):
        group = GROUPS[g]
        depth = sum(height(c) for c in group)
        rows = pl.ds(first_row(group[0]), depth)
        if part == 0:
            for c in group:
                for d in (0, 1, 3, 2):
                    tile = chi.at[other * 4 + ys_back[d], pl.ds(first_row(c), height(c)), :]
                    recv(tile, g_r.at[c, 4 + d]).wait_recv()
        for t in range(part * 8 // PARTS, (part + 1) * 8 // PARTS):
            s = pl.ds(t * LANES, LANES)
            update = jnp.dot(chi[t, rows, :].T, panel[rows, :], preferred_element_type=F32)
            if g == len(GROUPS) - 1:
                out[s, :] = (res[s, :].astype(F32) + (acc[s, :] + update)).astype(BF16)
            elif g == 0:
                acc[s, :] = update
            else:
                acc[s, :] += update

    steps = []

    def when(time, step, *args):
        steps.append((time, len(steps), functools.partial(step, *args)))

    for i, time in enumerate((7.2, 10.3, 12.8, 15.9, 19.4, 21.5, 25, 28, 30.8, 33.5)):
        when(time, crossed, i)
    for j, time in enumerate((5.6, 8.6, 11.8, 14.5, 17.4)):
        for block in (1, 2):
            k = j if block == 1 else SUBS - 1 - j
            if (k in ON_RIGHT[1]) == (block == 1):
                when(time, pass_on, block, k)
    for time, block, j in ((26.1, 5, 0), (32.2, 5, 1), (32.7, 6, 2), (34.8, 6, 3), (41.5, 6, 4)):
        when(time, pass_on, block, j)
    plan = (
        (8.7, 13.3, 19.5, 30.7, 36.5, 43.2),
        (17.5, 22, 33.6, 38.4, 43.3, 50),
        (26.2, 30.9, 37, 43.4, 47.2, 53.5),
        (34.9, 38.9, 44, 47.3, 51.2, 57),
        (41.6, 45.1, 49.8, 0, 54.5, 58.5),
        (44.1, 0, 50.1, 0, 54.7, 59),
        (45.5, 0, 51, 0, 55.1, 59.1),
    )
    for c, times in enumerate(plan):
        for time, step in zip(times, (multiply, scatter_y, scatter_z, gather_z, gather_y, gather_core), strict=True):
            if time:
                when(time, step, c)
    when(19.6, cross, 3)
    for g, times in enumerate(((47.4, 47.5, 49, 49.1), (51.1, 51.3, 52, 53), (55.2, 55.3, 55.4, 55.5), (58.6,) * 4, (60,) * 4)):
        for part, time in enumerate(times):
            when(time, multiply_back, g, part)

    cross(7)
    for j in range(SUBS):
        both_ways(0, j, SUBS - 1 - j)
    load_a.wait()
    load_r.wait()
    for _, _, step in sorted(steps, key=lambda s: s[:2]):
        step()
    for copy in unsent:
        copy.wait_send()


def cycle_term(amplitudes, residual_in, cholesky):
    dma = pltpu.SemaphoreType.DMA
    n = len(CHUNKS)
    any_space = pl.BlockSpec(memory_space=pl.ANY)
    return pl.pallas_call(
        body,
        name="cycle_term",
        out_shape=pltpu.VMEM((ROWS, COLS), BF16),
        in_specs=[any_space] * 3,
        out_specs=pl.BlockSpec(memory_space=pltpu.VMEM),
        scratch_shapes=[
            pltpu.VMEM((ROWS, COLS), BF16),
            pltpu.VMEM((ROWS, COLS), BF16),
            pltpu.VMEM((VEC, COLS), BF16),
            pltpu.VMEM((ROWS, COLS), F32),
            pltpu.VMEM((8, VEC, LANES), BF16),
            pltpu.VMEM((4, VEC, LANES), F32),
            pltpu.VMEM((4, VEC, LANES), F32),
            pltpu.VMEM((4, VEC, LANES), F32),
            pltpu.VMEM((8, VEC, LANES), BF16),
            pltpu.VMEM((8, VEC, LANES), BF16),
            pltpu.VMEM((VEC, LANES), F32),
            pltpu.VMEM((VEC, LANES), BF16),
            pltpu.VMEM((4, VEC, LANES), BF16),
            dma((2,)), dma((SUBS,)),
            dma((SLICES,)), dma((SLICES,)),
            dma((2, 2, SUBS)), dma((2, 2, SUBS)),
            dma((2, SUBS)), dma((2, SUBS)),
            dma((n,)), dma((n,)),
            dma((n, 8)), dma((n, 8)),
            dma((n, 4)), dma((n, 4)),
            dma((n, 4)), dma((n, 4)),
            dma((n, 8)), dma((n, 8)),
        ],
        compiler_params=pltpu.CompilerParams(collective_id=0, has_side_effects=True, vmem_limit_bytes=58 << 20),
        cost_estimate=pl.CostEstimate(flops=4 * ROWS * COLS * VEC, bytes_accessed=14 << 20, transcendentals=0),
    )(amplitudes, residual_in, cholesky.T)


def solution(mesh):
    in_specs = (P("row", "col"), P("row", "col"), P("col", "row"))
    out_specs = P("row", "col")
    return jax.shard_map(cycle_term, mesh=mesh, in_specs=in_specs, out_specs=out_specs, check_vma=False)
```

```python
import functools

import jax
import jax.numpy as jnp
from jax import lax
from jax.experimental import pallas as pl
from jax.experimental.pallas import tpu as pltpu
from jax.sharding import PartitionSpec as P

MESH = pl.DeviceIdType.MESH
BF16, F32 = jnp.bfloat16, jnp.float32

ROWS, COLS, VEC = 1024, 2048, 1280
SHARD = 160
SUBS, SUB = 5, 32
LANES = 128

ARRIVAL = (
    [(0, 0), (0, 1), (0, 2), (0, 3), (0, 4), (1, 0), (2, 4), (1, 1)]
    + [(2, 3), (1, 2), (2, 2), (1, 3), (2, 1), (1, 4), (2, 0), (4, 0)]
    + [(4, 1), (3, 0), (3, 4), (3, 1), (4, 2), (5, 0), (6, 0), (3, 3)]
    + [(3, 2), (4, 3), (5, 1), (6, 1), (5, 2), (6, 2), (6, 3), (4, 4)]
    + [(7, 0), (7, 2), (5, 3), (6, 4)]
    + [(7, 1), (7, 3)]
    + [(5, 4), (7, 4)]
)
PLACE = {piece: i * SUB for i, piece in enumerate(ARRIVAL)}
CHUNKS = (
    (8, False, False, False),
    (8, False, False, False),
    (8, False, False, False),
    (4, False, False, False),
    (4, True, False, False),
    (2, False, True, False),
    (2, False, True, False),
    (2, False, True, False),
    (2, True, True, True),
)
STARTS = [sum(chunk[0] for chunk in CHUNKS[:i]) for i in range(len(CHUNKS))]
GROUPS = ((0,), (1,), (2,), (3, 4), (5, 6, 7, 8))
PARTS = 4
SLICES, SLICE = 10, 16
ON_RIGHT = {1: (0, 1, 2), 5: (0, 1)}


def first_row(chunk):
    return STARTS[chunk] * SUB


def height(chunk):
    return CHUNKS[chunk][0] * SUB


def body(
    a_hbm, r_hbm, c_hbm, out,
    a, a_turned, res, panel, acc, chi, own, sib_out, sib_in, y_out, y_in, y_sum, z_out, z_in,
    local_sem, own_sem, zx_s, zx_r, x_s, x_r, f_s, f_r, core_s, core_r, y_s, y_r, z_s, z_r, zg_s, zg_r, g_s, g_r,
):
    row, col = lax.axis_index("row"), lax.axis_index("col")
    y, zl, core = col // 8, lax.rem(col // 2, 4), lax.rem(col, 2)
    other = 1 - core

    def at(y, zl, core):
        return (row, (y * 4 + zl) * 2 + core)

    right, left = (lax.rem(row + 2, 8), col), (lax.rem(row + 6, 8), col)
    across = (row + 1 - 2 * lax.rem(row, 2), col)
    sibling = at(y, zl, other)
    ys = [lax.rem(y + d, 4) for d in range(4)]
    ys_back = [lax.rem(y + 4 - d, 4) for d in range(4)]
    zs = [lax.rem(zl + e, 4) for e in range(4)]
    partners = [across, right, left]
    partners += [at(ys[d], zl, core) for d in (1, 2, 3)]
    partners += [at(ys[d], zl, other) for d in (1, 2, 3)]
    partners += [at(y, zs[e], core) for e in (1, 2, 3)]
    partners += [sibling]

    barrier = pltpu.get_barrier_semaphore()
    for device in partners:
        pl.semaphore_signal(barrier, inc=1, device_id=device, device_id_type=MESH)
    load_c = [
        pltpu.make_async_copy(c_hbm.at[pl.ds(j * SUB, SUB), :], panel.at[pl.ds(PLACE[0, j], SUB), :], own_sem.at[j])
        for j in range(SUBS)
    ]
    load_a = pltpu.make_async_copy(a_hbm, a, local_sem.at[0])
    load_r = pltpu.make_async_copy(r_hbm, res, local_sem.at[1])
    for load in load_c:
        load.start()
    load_a.start()
    load_r.start()
    pl.semaphore_wait(barrier, len(partners))

    unsent = []

    def send(src, dst, send_sem, recv_sem, device):
        copy = pltpu.make_async_remote_copy(
            src_ref=src, dst_ref=dst, send_sem=send_sem, recv_sem=recv_sem, device_id=device, device_id_type=MESH
        )
        copy.start()
        unsent.append(copy)
        return copy

    arriving = {}

    def move(piece, to, send_sem, recv_sem, device):
        block, j = piece
        src = panel.at[pl.ds(PLACE[piece], SUB), :] if block else c_hbm.at[pl.ds(j * SUB, SUB), :]
        arriving[to] = send(
            src, panel.at[pl.ds(PLACE[to], SUB), :], send_sem, recv_sem, device
        )

    def need(piece):
        if piece in arriving:
            arriving.pop(piece).wait_recv()

    crossing = []

    def cross(count):
        for i in range(len(crossing), len(crossing) + count):
            j, offset = i * SLICE // SUB, i * SLICE % SUB
            src, dst = pl.ds(i * SLICE, SLICE), pl.ds(PLACE[4, j] + offset, SLICE)
            crossing.append(send(c_hbm.at[src, :], panel.at[dst, :], zx_s.at[i], zx_r.at[i], across))

    def crossed(i):
        crossing[i].wait_recv()
        j, offset = i * SLICE // SUB, i * SLICE % SUB
        if offset + SLICE == SUB:
            both_ways(4, j, j)

    def both_ways(block, j, jl):
        which = block // 4
        move((block, j), (block + 1, j), x_s.at[which, 0, j], x_r.at[which, 0, j], right)
        move((block, jl), (block + 2, jl), x_s.at[which, 1, jl], x_r.at[which, 1, jl], left)

    def pass_on(block, j):
        need((block, j))
        base = 1 if block < 4 else 5
        goes_right = j in ON_RIGHT[base]
        if goes_right == (block == base):
            device = right if goes_right else left
            move((block, j), (base + 2, j), f_s.at[base // 4, j], f_r.at[base // 4, j], device)

    def multiply(c):
        n, direct, _, _ = CHUNKS[c]
        for piece in ARRIVAL[STARTS[c] : STARTS[c] + n]:
            need(piece)
        rows = pl.ds(first_row(c), height(c))

        def half(which, into):
            s = pl.ds(pl.multiple_of(which * 512, 512), 512)
            part = jnp.dot(panel[rows, :], a_turned[:, s], preferred_element_type=F32)
            for t in range(4):
                tile = part[:, t * LANES : (t + 1) * LANES]
                into[t, rows, :] = tile
                if direct:
                    y_out[which * 4 + t, rows, :] = tile.astype(BF16)

        half(other, sib_out)
        if direct:
            for d in (2, 1, 3, 0):
                send(
                    y_out.at[other * 4 + ys[d], rows, :], y_in.at[4 + d, rows, :],
                    y_s.at[c, 4 + d], y_r.at[c, 4 + d], at(ys[d], zl, other),
                )
        else:
            core_copies[c] = send(sib_out.at[:, rows, :], sib_in.at[:, rows, :], core_s.at[c], core_r.at[c], sibling)
        half(core, own)
        if direct:
            for d in (2, 1, 3):
                send_y(c, rows, d)

    core_copies = {}

    def recv(dst, sem):
        return pltpu.make_async_remote_copy(
            src_ref=dst, dst_ref=dst, send_sem=sem, recv_sem=sem, device_id=sibling, device_id_type=MESH
        )

    def send_y(c, rows, d):
        send(
            y_out.at[core * 4 + ys[d], rows, :], y_in.at[d, rows, :],
            y_s.at[c, d], y_r.at[c, d], at(ys[d], zl, core),
        )

    def scatter_y(c):
        if CHUNKS[c][1]:
            return
        rows = pl.ds(first_row(c), height(c))
        core_copies[c].wait_recv()
        for d in (2, 1, 3, 0):
            total = own[ys[d], rows, :] + sib_in[ys[d], rows, :]
            if d:
                y_out[core * 4 + ys[d], rows, :] = total.astype(BF16)
                send_y(c, rows, d)
            else:
                own[y, rows, :] = total

    def scatter_z(c):
        rows = pl.ds(first_row(c), height(c))
        part = height(c) // 4
        total = own[y, rows, :]
        for d in (1, 3, 2, 4, 5, 7, 6) if CHUNKS[c][1] else (1, 3, 2):
            recv(y_in.at[d, rows, :], y_r.at[c, d]).wait_recv()
            total = total + y_in[d, rows, :].astype(F32)
        y_sum[rows, :] = total
        z_out[rows, :] = total.astype(BF16)
        if CHUNKS[c][2]:
            for e in (3, 2, 1):
                send(z_out.at[rows, :], z_in.at[e, rows, :], z_s.at[c, e], z_r.at[c, e], at(y, zs[e], core))
            return
        for e in (3, 2, 1):
            src = pl.ds(pl.multiple_of(first_row(c) + part * zs[e], 16), part)
            dst = pl.ds(first_row(c) // 4, part)
            send(z_out.at[src, :], z_in.at[e, dst, :], z_s.at[c, e], z_r.at[c, e], at(y, zs[e], core))

    def gather_z(c):
        if CHUNKS[c][2]:
            return
        part = height(c) // 4
        mine = pl.ds(pl.multiple_of(first_row(c) + part * zl, 16), part)
        total = y_sum[mine, :]
        for e in (1, 2, 3):
            slot = pl.ds(first_row(c) // 4, part)
            recv(z_in.at[e, slot, :], z_r.at[c, e]).wait_recv()
            total = total + z_in[e, slot, :].astype(F32)
        tile = core * 4 + y
        chi[tile, mine, :] = total.astype(BF16)
        for e in (3, 2, 1):
            piece = chi.at[tile, mine, :]
            send(piece, piece, zg_s.at[c, e], zg_r.at[c, e], at(y, zs[e], core))

    def gather_y(c):
        rows = pl.ds(first_row(c), height(c))
        part = height(c) // 4
        tile = chi.at[core * 4 + y, rows, :]
        if CHUNKS[c][2]:
            total = y_sum[rows, :]
            for e in (1, 2, 3):
                recv(z_in.at[e, rows, :], z_r.at[c, e]).wait_recv()
                total = total + z_in[e, rows, :].astype(F32)
            chi[core * 4 + y, rows, :] = total.astype(BF16)
        for e in () if CHUNKS[c][2] else (1, 2, 3):
            theirs = pl.ds(pl.multiple_of(first_row(c) + part * lax.rem(zl + 4 - e, 4), 16), part)
            recv(chi.at[core * 4 + y, theirs, :], zg_r.at[c, e]).wait_recv()
        for d in (2, 1, 3):
            send(tile, tile, g_s.at[c, d], g_r.at[c, d], at(ys[d], zl, core))
            if CHUNKS[c][3]:
                send(tile, tile, g_s.at[c, 4 + d], g_r.at[c, 4 + d], at(ys[d], zl, other))
        send(tile, tile, g_s.at[c, 4], g_r.at[c, 4], sibling)

    def gather_core(c):
        rows = pl.ds(first_row(c), height(c))
        for d in (1, 3, 2):
            tile = chi.at[core * 4 + ys_back[d], rows, :]
            recv(tile, g_r.at[c, d]).wait_recv()
            if not CHUNKS[c][3]:
                send(tile, tile, g_s.at[c, 4 + d], g_r.at[c, 4 + d], sibling)

    def multiply_back(g, part):
        group = GROUPS[g]
        depth = sum(height(c) for c in group)
        rows = pl.ds(first_row(group[0]), depth)
        if part == 0:
            for c in group:
                for d in (0, 1, 3, 2):
                    tile = chi.at[other * 4 + ys_back[d], pl.ds(first_row(c), height(c)), :]
                    recv(tile, g_r.at[c, 4 + d]).wait_recv()
        for t in range(part * 8 // PARTS, (part + 1) * 8 // PARTS):
            s = pl.ds(t * LANES, LANES)
            update = jnp.dot(chi[t, rows, :].T, panel[rows, :], preferred_element_type=F32)
            if g == len(GROUPS) - 1:
                out[s, :] = (res[s, :].astype(F32) + (acc[s, :] + update)).astype(BF16)
            elif g == 0:
                acc[s, :] = update
            else:
                acc[s, :] += update

    cross(10)
    for j in range(SUBS):
        both_ways(0, j, SUBS - 1 - j)
    for load in load_c:
        load.wait()
    load_a.wait()
    load_r.wait()

    @pl.loop(0, ROWS // LANES)
    def _(t):
        s = pl.ds(pl.multiple_of(t * LANES, LANES), LANES)
        a_turned[:, s] = a[s, :].T

    pass_on(1, 0)
    pass_on(2, 4)
    crossed(0)
    pass_on(1, 1)
    pass_on(2, 3)
    multiply(0)
    crossed(1)
    pass_on(1, 2)
    scatter_y(0)
    crossed(2)
    crossed(3)
    multiply(1)
    crossed(4)
    scatter_z(0)
    scatter_y(1)
    crossed(5)
    crossed(6)
    pass_on(5, 0)
    multiply(2)
    crossed(7)
    scatter_z(1)
    scatter_y(2)
    crossed(8)
    pass_on(5, 1)
    pass_on(6, 2)
    multiply(3)
    crossed(9)
    gather_z(0)
    scatter_y(3)
    pass_on(6, 3)
    multiply(4)
    scatter_z(2)
    gather_z(1)
    multiply(5)
    gather_y(0)
    scatter_z(3)
    scatter_y(5)
    pass_on(6, 4)
    multiply(6)
    gather_z(2)
    scatter_z(4)
    gather_y(1)
    scatter_y(6)
    gather_z(3)
    multiply(7)
    gather_core(0)
    scatter_z(5)
    scatter_y(7)
    multiply(8)
    gather_z(4)
    gather_y(2)
    gather_core(1)
    multiply_back(0, 0)
    gather_y(3)
    scatter_z(6)
    multiply_back(0, 1)
    multiply_back(0, 2)
    multiply_back(0, 3)
    scatter_z(7)
    multiply_back(1, 0)
    multiply_back(1, 1)
    gather_y(4)
    scatter_z(8)
    multiply_back(1, 2)
    multiply_back(1, 3)
    gather_y(5)
    gather_y(6)
    gather_core(2)
    gather_y(7)
    gather_core(3)
    multiply_back(2, 0)
    gather_y(8)
    multiply_back(2, 1)
    multiply_back(2, 2)
    gather_core(4)
    multiply_back(2, 3)
    gather_core(5)
    gather_core(6)
    multiply_back(3, 0)
    gather_core(7)
    multiply_back(3, 1)
    multiply_back(3, 2)
    multiply_back(3, 3)
    gather_core(8)
    multiply_back(4, 0)
    multiply_back(4, 1)
    multiply_back(4, 2)
    multiply_back(4, 3)
    for copy in unsent:
        copy.wait_send()


def cycle_term(amplitudes, residual_in, cholesky):
    dma = pltpu.SemaphoreType.DMA
    n = len(CHUNKS)
    any_space = pl.BlockSpec(memory_space=pl.ANY)
    return pl.pallas_call(
        body,
        name="cycle_term",
        out_shape=pltpu.VMEM((ROWS, COLS), BF16),
        in_specs=[any_space] * 3,
        out_specs=pl.BlockSpec(memory_space=pltpu.VMEM),
        scratch_shapes=[
            pltpu.VMEM((ROWS, COLS), BF16),
            pltpu.VMEM((COLS, ROWS), BF16),
            pltpu.VMEM((ROWS, COLS), BF16),
            pltpu.VMEM((VEC, COLS), BF16),
            pltpu.VMEM((ROWS, COLS), F32),
            pltpu.VMEM((8, VEC, LANES), BF16),
            pltpu.VMEM((4, VEC, LANES), F32),
            pltpu.VMEM((4, VEC, LANES), F32),
            pltpu.VMEM((4, VEC, LANES), F32),
            pltpu.VMEM((8, VEC, LANES), BF16),
            pltpu.VMEM((8, VEC, LANES), BF16),
            pltpu.VMEM((VEC, LANES), F32),
            pltpu.VMEM((VEC, LANES), BF16),
            pltpu.VMEM((4, VEC, LANES), BF16),
            dma((2,)), dma((SUBS,)),
            dma((SLICES,)), dma((SLICES,)),
            dma((2, 2, SUBS)), dma((2, 2, SUBS)),
            dma((2, SUBS)), dma((2, SUBS)),
            dma((n,)), dma((n,)),
            dma((n, 8)), dma((n, 8)),
            dma((n, 4)), dma((n, 4)),
            dma((n, 4)), dma((n, 4)),
            dma((n, 8)), dma((n, 8)),
        ],
        compiler_params=pltpu.CompilerParams(collective_id=0, has_side_effects=True, vmem_limit_bytes=58 << 20),
        cost_estimate=pl.CostEstimate(flops=4 * ROWS * COLS * VEC, bytes_accessed=14 << 20, transcendentals=0),
    )(amplitudes, residual_in, cholesky.T)


def solution(mesh):
    in_specs = (P("row", "col"), P("row", "col"), P("col", "row"))
    out_specs = P("row", "col")
    return jax.shard_map(cycle_term, mesh=mesh, in_specs=in_specs, out_specs=out_specs, check_vma=False)
```

```python
import functools

import jax
import jax.numpy as jnp
from jax import lax
from jax.experimental import pallas as pl
from jax.experimental.pallas import tpu as pltpu
from jax.sharding import PartitionSpec as P

MESH = pl.DeviceIdType.MESH
BF16, F32 = jnp.bfloat16, jnp.float32

ROWS, COLS, VEC = 1024, 2048, 1280
SHARD = 160
SUBS, SUB = 5, 32
LANES = 128

ARRIVAL = (
    [(0, 0), (0, 1), (0, 2), (0, 3), (0, 4), (1, 0), (2, 4), (1, 1)]
    + [(2, 3), (1, 2), (2, 2), (1, 3), (2, 1), (1, 4), (2, 0), (4, 0)]
    + [(4, 1), (3, 0), (3, 4), (3, 1), (4, 2), (5, 0), (6, 0), (3, 3)]
    + [(3, 2), (4, 3), (5, 1), (6, 1), (5, 2), (6, 2), (6, 3), (4, 4)]
    + [(7, 0), (7, 2), (5, 3), (6, 4)]
    + [(7, 1), (7, 3)]
    + [(5, 4), (7, 4)]
)
PLACE = {piece: i * SUB for i, piece in enumerate(ARRIVAL)}
CHUNKS = (
    (8, False, False, False),
    (8, False, False, False),
    (8, False, False, False),
    (4, False, False, False),
    (4, True, False, False),
    (2, False, True, False),
    (2, False, True, False),
    (2, False, True, False),
    (2, True, True, True),
)
STARTS = [sum(chunk[0] for chunk in CHUNKS[:i]) for i in range(len(CHUNKS))]
GROUPS = ((0,), (1,), (2,), (3, 4), (5, 6, 7, 8))
PARTS = 4
SLICES, SLICE = 10, 16
ON_RIGHT = {1: (0, 1, 2), 5: (0, 1)}


def first_row(chunk):
    return STARTS[chunk] * SUB


def height(chunk):
    return CHUNKS[chunk][0] * SUB


def body(
    a_hbm, r_hbm, c_hbm, out,
    a, a_turned, res, panel, acc, chi, own, sib_out, sib_in, y_out, y_in, y_sum, z_out, z_in,
    local_sem, own_sem, zx_s, zx_r, x_s, x_r, f_s, f_r, core_s, core_r, y_s, y_r, z_s, z_r, zg_s, zg_r, g_s, g_r,
):
    row, col = lax.axis_index("row"), lax.axis_index("col")
    y, zl, core = col // 8, lax.rem(col // 2, 4), lax.rem(col, 2)
    other = 1 - core

    def at(y, zl, core):
        return (row, (y * 4 + zl) * 2 + core)

    right, left = (lax.rem(row + 2, 8), col), (lax.rem(row + 6, 8), col)
    across = (row + 1 - 2 * lax.rem(row, 2), col)
    sibling = at(y, zl, other)
    ys = [lax.rem(y + d, 4) for d in range(4)]
    ys_back = [lax.rem(y + 4 - d, 4) for d in range(4)]
    zs = [lax.rem(zl + e, 4) for e in range(4)]
    partners = [across, right, left]
    partners += [at(ys[d], zl, core) for d in (1, 2, 3)]
    partners += [at(ys[d], zl, other) for d in (1, 2, 3)]
    partners += [at(y, zs[e], core) for e in (1, 2, 3)]
    partners += [sibling]

    barrier = pltpu.get_barrier_semaphore()
    for device in partners:
        pl.semaphore_signal(barrier, inc=1, device_id=device, device_id_type=MESH)
    load_c = [
        pltpu.make_async_copy(c_hbm.at[pl.ds(j * SUB, SUB), :], panel.at[pl.ds(PLACE[0, j], SUB), :], own_sem.at[j])
        for j in range(SUBS)
    ]
    load_a = pltpu.make_async_copy(a_hbm, a, local_sem.at[0])
    load_r = pltpu.make_async_copy(r_hbm, res, local_sem.at[1])
    for load in load_c:
        load.start()
    load_a.start()
    load_r.start()
    pl.semaphore_wait(barrier, len(partners))

    unsent = []

    def send(src, dst, send_sem, recv_sem, device):
        copy = pltpu.make_async_remote_copy(
            src_ref=src, dst_ref=dst, send_sem=send_sem, recv_sem=recv_sem, device_id=device, device_id_type=MESH
        )
        copy.start()
        unsent.append(copy)
        return copy

    def drain(count):
        for _ in range(count):
            unsent.pop(0).wait_send()

    arriving = {}

    def move(piece, to, send_sem, recv_sem, device):
        block, j = piece
        src = panel.at[pl.ds(PLACE[piece], SUB), :] if block else c_hbm.at[pl.ds(j * SUB, SUB), :]
        arriving[to] = send(
            src, panel.at[pl.ds(PLACE[to], SUB), :], send_sem, recv_sem, device
        )

    def need(piece):
        if piece in arriving:
            arriving.pop(piece).wait_recv()

    crossing = []

    def cross(count):
        for i in range(len(crossing), len(crossing) + count):
            j, offset = i * SLICE // SUB, i * SLICE % SUB
            src, dst = pl.ds(i * SLICE, SLICE), pl.ds(PLACE[4, j] + offset, SLICE)
            crossing.append(send(c_hbm.at[src, :], panel.at[dst, :], zx_s.at[i], zx_r.at[i], across))

    def crossed(i):
        crossing[i].wait_recv()
        j, offset = i * SLICE // SUB, i * SLICE % SUB
        if offset + SLICE == SUB:
            both_ways(4, j, j)

    def both_ways(block, j, jl):
        which = block // 4
        move((block, j), (block + 1, j), x_s.at[which, 0, j], x_r.at[which, 0, j], right)
        move((block, jl), (block + 2, jl), x_s.at[which, 1, jl], x_r.at[which, 1, jl], left)

    def pass_on(block, j):
        need((block, j))
        base = 1 if block < 4 else 5
        goes_right = j in ON_RIGHT[base]
        if goes_right == (block == base):
            device = right if goes_right else left
            move((block, j), (base + 2, j), f_s.at[base // 4, j], f_r.at[base // 4, j], device)

    def multiply(c):
        n, direct, _, _ = CHUNKS[c]
        for piece in ARRIVAL[STARTS[c] : STARTS[c] + n]:
            need(piece)
        rows = pl.ds(first_row(c), height(c))

        def half(which, into):
            s = pl.ds(pl.multiple_of(which * 512, 512), 512)
            part = jnp.dot(panel[rows, :], a_turned[:, s], preferred_element_type=F32)
            for t in range(4):
                tile = part[:, t * LANES : (t + 1) * LANES]
                into[t, rows, :] = tile
                if direct:
                    y_out[which * 4 + t, rows, :] = tile.astype(BF16)

        half(other, sib_out)
        if direct:
            for d in (2, 1, 3, 0):
                send(
                    y_out.at[other * 4 + ys[d], rows, :], y_in.at[4 + d, rows, :],
                    y_s.at[c, 4 + d], y_r.at[c, 4 + d], at(ys[d], zl, other),
                )
        else:
            core_copies[c] = send(sib_out.at[:, rows, :], sib_in.at[:, rows, :], core_s.at[c], core_r.at[c], sibling)
        half(core, own)
        if direct:
            for d in (2, 1, 3):
                send_y(c, rows, d)

    core_copies = {}

    def recv(dst, sem):
        return pltpu.make_async_remote_copy(
            src_ref=dst, dst_ref=dst, send_sem=sem, recv_sem=sem, device_id=sibling, device_id_type=MESH
        )

    def send_y(c, rows, d):
        send(
            y_out.at[core * 4 + ys[d], rows, :], y_in.at[d, rows, :],
            y_s.at[c, d], y_r.at[c, d], at(ys[d], zl, core),
        )

    def scatter_y(c):
        if CHUNKS[c][1]:
            return
        rows = pl.ds(first_row(c), height(c))
        core_copies[c].wait_recv()
        for d in (2, 1, 3, 0):
            total = own[ys[d], rows, :] + sib_in[ys[d], rows, :]
            if d:
                y_out[core * 4 + ys[d], rows, :] = total.astype(BF16)
                send_y(c, rows, d)
            else:
                own[y, rows, :] = total

    def scatter_z(c):
        rows = pl.ds(first_row(c), height(c))
        part = height(c) // 4
        total = own[y, rows, :]
        for d in (1, 3, 2, 4, 5, 7, 6) if CHUNKS[c][1] else (1, 3, 2):
            recv(y_in.at[d, rows, :], y_r.at[c, d]).wait_recv()
            total = total + y_in[d, rows, :].astype(F32)
        y_sum[rows, :] = total
        z_out[rows, :] = total.astype(BF16)
        if CHUNKS[c][2]:
            for e in (3, 2, 1):
                send(z_out.at[rows, :], z_in.at[e, rows, :], z_s.at[c, e], z_r.at[c, e], at(y, zs[e], core))
            return
        for e in (3, 2, 1):
            src = pl.ds(pl.multiple_of(first_row(c) + part * zs[e], 16), part)
            dst = pl.ds(first_row(c) // 4, part)
            send(z_out.at[src, :], z_in.at[e, dst, :], z_s.at[c, e], z_r.at[c, e], at(y, zs[e], core))

    def gather_z(c):
        if CHUNKS[c][2]:
            return
        part = height(c) // 4
        mine = pl.ds(pl.multiple_of(first_row(c) + part * zl, 16), part)
        total = y_sum[mine, :]
        for e in (1, 2, 3):
            slot = pl.ds(first_row(c) // 4, part)
            recv(z_in.at[e, slot, :], z_r.at[c, e]).wait_recv()
            total = total + z_in[e, slot, :].astype(F32)
        tile = core * 4 + y
        chi[tile, mine, :] = total.astype(BF16)
        for e in (3, 2, 1):
            piece = chi.at[tile, mine, :]
            send(piece, piece, zg_s.at[c, e], zg_r.at[c, e], at(y, zs[e], core))

    def gather_y(c):
        rows = pl.ds(first_row(c), height(c))
        part = height(c) // 4
        tile = chi.at[core * 4 + y, rows, :]
        if CHUNKS[c][2]:
            total = y_sum[rows, :]
            for e in (1, 2, 3):
                recv(z_in.at[e, rows, :], z_r.at[c, e]).wait_recv()
                total = total + z_in[e, rows, :].astype(F32)
            chi[core * 4 + y, rows, :] = total.astype(BF16)
        for e in () if CHUNKS[c][2] else (1, 2, 3):
            theirs = pl.ds(pl.multiple_of(first_row(c) + part * lax.rem(zl + 4 - e, 4), 16), part)
            recv(chi.at[core * 4 + y, theirs, :], zg_r.at[c, e]).wait_recv()
        for d in (2, 1, 3):
            send(tile, tile, g_s.at[c, d], g_r.at[c, d], at(ys[d], zl, core))
            if CHUNKS[c][3]:
                send(tile, tile, g_s.at[c, 4 + d], g_r.at[c, 4 + d], at(ys[d], zl, other))
        send(tile, tile, g_s.at[c, 4], g_r.at[c, 4], sibling)

    def gather_core(c):
        rows = pl.ds(first_row(c), height(c))
        for d in (1, 3, 2):
            tile = chi.at[core * 4 + ys_back[d], rows, :]
            recv(tile, g_r.at[c, d]).wait_recv()
            if not CHUNKS[c][3]:
                send(tile, tile, g_s.at[c, 4 + d], g_r.at[c, 4 + d], sibling)

    def multiply_back(g, part):
        group = GROUPS[g]
        depth = sum(height(c) for c in group)
        rows = pl.ds(first_row(group[0]), depth)
        if part == 0:
            for c in group:
                for d in (0, 1, 3, 2):
                    tile = chi.at[other * 4 + ys_back[d], pl.ds(first_row(c), height(c)), :]
                    recv(tile, g_r.at[c, 4 + d]).wait_recv()
        for t in range(part * 8 // PARTS, (part + 1) * 8 // PARTS):
            s = pl.ds(t * LANES, LANES)
            update = jnp.dot(chi[t, rows, :].T, panel[rows, :], preferred_element_type=F32)
            if g == len(GROUPS) - 1:
                out[s, :] = (acc[s, :] + update).astype(BF16)
            elif g == 0:
                acc[s, :] = res[s, :].astype(F32) + update
            else:
                acc[s, :] += update

    cross(10)
    for j in range(SUBS):
        both_ways(0, j, SUBS - 1 - j)
    for load in load_c:
        load.wait()
    load_a.wait()
    load_r.wait()

    @pl.loop(0, ROWS // LANES)
    def _(t):
        s = pl.ds(pl.multiple_of(t * LANES, LANES), LANES)
        a_turned[:, s] = a[s, :].T

    pass_on(1, 0)
    pass_on(2, 4)
    crossed(0)
    pass_on(1, 1)
    pass_on(2, 3)
    multiply(0)
    crossed(1)
    pass_on(1, 2)
    scatter_y(0)
    crossed(2)
    crossed(3)
    multiply(1)
    early = len(unsent)
    crossed(4)
    scatter_z(0)
    scatter_y(1)
    crossed(5)
    crossed(6)
    pass_on(5, 0)
    multiply(2)
    crossed(7)
    scatter_z(1)
    scatter_y(2)
    crossed(8)
    pass_on(5, 1)
    pass_on(6, 2)
    multiply(3)
    drain(early)
    crossed(9)
    gather_z(0)
    scatter_y(3)
    pass_on(6, 3)
    multiply(4)
    scatter_z(2)
    gather_z(1)
    multiply(5)
    middle = len(unsent)
    gather_y(0)
    scatter_z(3)
    scatter_y(5)
    pass_on(6, 4)
    multiply(6)
    gather_z(2)
    scatter_z(4)
    gather_y(1)
    scatter_y(6)
    gather_z(3)
    multiply(7)
    gather_core(0)
    scatter_z(5)
    scatter_y(7)
    multiply(8)
    gather_z(4)
    gather_y(2)
    gather_core(1)
    multiply_back(0, 0)
    gather_y(3)
    scatter_z(6)
    multiply_back(0, 1)
    multiply_back(0, 2)
    multiply_back(0, 3)
    scatter_z(7)
    multiply_back(1, 0)
    multiply_back(1, 1)
    gather_y(4)
    scatter_z(8)
    multiply_back(1, 2)
    multiply_back(1, 3)
    gather_y(5)
    gather_y(6)
    drain(middle)
    gather_core(2)
    gather_y(7)
    gather_core(3)
    multiply_back(2, 0)
    gather_y(8)
    multiply_back(2, 1)
    multiply_back(2, 2)
    gather_core(4)
    multiply_back(2, 3)
    gather_core(5)
    gather_core(6)
    multiply_back(3, 0)
    gather_core(7)
    multiply_back(3, 1)
    multiply_back(3, 2)
    multiply_back(3, 3)
    gather_core(8)
    multiply_back(4, 0)
    multiply_back(4, 1)
    multiply_back(4, 2)
    multiply_back(4, 3)
    for copy in unsent:
        copy.wait_send()


def cycle_term(amplitudes, residual_in, cholesky):
    dma = pltpu.SemaphoreType.DMA
    n = len(CHUNKS)
    any_space = pl.BlockSpec(memory_space=pl.ANY)
    return pl.pallas_call(
        body,
        name="cycle_term",
        out_shape=pltpu.VMEM((ROWS, COLS), BF16),
        in_specs=[any_space] * 3,
        out_specs=pl.BlockSpec(memory_space=pltpu.VMEM),
        scratch_shapes=[
            pltpu.VMEM((ROWS, COLS), BF16),
            pltpu.VMEM((COLS, ROWS), BF16),
            pltpu.VMEM((ROWS, COLS), BF16),
            pltpu.VMEM((VEC, COLS), BF16),
            pltpu.VMEM((ROWS, COLS), F32),
            pltpu.VMEM((8, VEC, LANES), BF16),
            pltpu.VMEM((4, VEC, LANES), F32),
            pltpu.VMEM((4, VEC, LANES), F32),
            pltpu.VMEM((4, VEC, LANES), F32),
            pltpu.VMEM((8, VEC, LANES), BF16),
            pltpu.VMEM((8, VEC, LANES), BF16),
            pltpu.VMEM((VEC, LANES), F32),
            pltpu.VMEM((VEC, LANES), BF16),
            pltpu.VMEM((4, VEC, LANES), BF16),
            dma((2,)), dma((SUBS,)),
            dma((SLICES,)), dma((SLICES,)),
            dma((2, 2, SUBS)), dma((2, 2, SUBS)),
            dma((2, SUBS)), dma((2, SUBS)),
            dma((n,)), dma((n,)),
            dma((n, 8)), dma((n, 8)),
            dma((n, 4)), dma((n, 4)),
            dma((n, 4)), dma((n, 4)),
            dma((n, 8)), dma((n, 8)),
        ],
        compiler_params=pltpu.CompilerParams(collective_id=0, has_side_effects=True, vmem_limit_bytes=58 << 20),
        cost_estimate=pl.CostEstimate(flops=4 * ROWS * COLS * VEC, bytes_accessed=14 << 20, transcendentals=0),
    )(amplitudes, residual_in, cholesky.T)


def solution(mesh):
    in_specs = (P("row", "col"), P("row", "col"), P("col", "row"))
    out_specs = P("row", "col")
    return jax.shard_map(cycle_term, mesh=mesh, in_specs=in_specs, out_specs=out_specs, check_vma=False)
```
